256 devices in a mesh: depth: 4 (over z_hi), row: 4 (over x), col: 16 (over z_lo, y, core).
Axes of the slice: x: 4, y: 4, z: 8 (z_hi: 4, z_lo: 2; z = z_hi * 2 + z_lo), core: 2. Of those that a mesh axis runs over, the one named last changes fastest.
Arguments:
- activations: bfloat16 [2048, 12288], P(('depth', 'col'), 'row'), may hold values from -0.625 to 0.625
- out_grad: bfloat16 [2048, 18432], P(('depth', 'row'), 'col'), may hold values from -6 to 6
- weight: bfloat16 [12288, 18432], P('row', 'col'), may hold values from -0.078125 to 0.078125
Outputs:
- input_grad: bfloat16 [2048, 12288], P('depth', ('row', 'col'))
- weight_grad: float32 [4, 4, 768, 18432], P('row', 'depth', None, 'col')
The draws below stay inside these ranges and needn't reach their ends.
All inputs are finite; a program needn't handle non-finite values.
Results may differ from the reference program's by a relative error of at most 0.001.
Values may be sent and summed in bfloat16 or wider, within the bound.
A program may use at most 128 MiB of HBM per device.

```python
import jax
import jax.numpy as jnp
from jax import lax

D = 12288
F = 18432
TOKENS = 2048
N_DEPTH = 4
N_ROW = 4


def spiked(drawn, own_key, source, target, parts, factor):
    def block_of(dim):
        return (jnp.arange(drawn.shape[dim]) // (drawn.shape[dim] // parts)).reshape((-1,) + (1,) * (drawn.ndim - 1 - dim))

    first = jax.random.permutation(own_key, parts)[block_of(target)]
    second = (block_of(target) + parts // 2) % parts
    return jnp.where((block_of(source) == first) | (block_of(source) == second), factor * drawn, drawn)


def shard_levels(stream_key, dims, shards, smallest, top_value):
    factor_of = 1.0
    for dim, shards_of in shards:
        heights = jax.random.uniform(jax.random.fold_in(jax.random.fold_in(stream_key, 6), dim), (shards_of,), jnp.float32, smallest / len(shards), top_value / len(shards))
        factor_of = factor_of * jnp.repeat(jnp.exp(heights), dims[dim] // shards_of).reshape((-1,) + (1,) * (len(dims) - 1 - dim))
    return factor_of


def noise(key, extent, width, most, shards=(), held_as=jnp.bfloat16):
    result = jax.random.normal(key, extent, jnp.float32) * width
    if len(shards) > 0:
        result = shard_levels(key, extent, shards, -0.22, 0.18) * result
    return jnp.clip(result, min=-most, max=most).astype(held_as)


def gaussian_with(own_key, shape, deviation, reach, shards, heavy, held_as=jnp.bfloat16):
    entries = deviation * jax.random.normal(own_key, shape, jnp.float32)
    if shards:
        entries = entries * shard_levels(own_key, shape, shards, -0.22, 0.18)
    return jnp.clip(spiked(entries, jax.random.fold_in(own_key, 3), *heavy), -reach, reach).astype(held_as)


def setup_inputs(seed: int = 0) -> dict:
    keys = jax.random.split(jax.random.key(seed), 4)
    activations = noise(keys[0], (TOKENS, D), (2.0 / TOKENS ** 0.5), 0.625, ((0, 64), (1, 4)))
    out_grad = noise(keys[1], (TOKENS, F), 1.0, 6.0, ((0, 16), (1, 16)))
    weight = gaussian_with(keys[2], (D, F), D ** -0.5, 0.078125, ((0, 4), (1, 16)), (1, 0, 16, 2.0))
    return dict(activations=activations, out_grad=out_grad, weight=weight)


def reference(activations, out_grad, weight):
    input_total = lax.dot_general(out_grad, weight, (((1,), (1,)), ((), ())), preferred_element_type=jnp.float32)
    weight_total = lax.dot_general(activations, out_grad, (((0,), (0,)), ((), ())), preferred_element_type=jnp.float32)
    weight_grad = weight_total.reshape(N_ROW, N_DEPTH, D // (N_ROW * N_DEPTH), F)
    return input_total.astype(jnp.bfloat16), weight_grad
```

```python
import jax
import jax.numpy as jnp
from jax import lax
from jax.experimental import pallas as pl
from jax.experimental.pallas import tpu as pltpu
from jax.sharding import PartitionSpec as P

F32 = jnp.float32
BF16 = jnp.bfloat16
SEMS = 112


def kernel(act, og, wt, ig_out, wg_out, W, OG, OGP, ACT, PT, R1, R2, SZ, RZ, FN, ACC, ssem, rsem, lsem):
    h = lax.axis_index("depth")
    x = lax.axis_index("row")
    c = lax.axis_index("col")
    k = lax.rem(c, 2)
    y = lax.rem(lax.div(c, 2), 4)
    l = lax.div(c, 8)
    ok, ol = 1 - k, 1 - l
    up = lambda v: lax.rem(v + 1, 4)
    dn = lambda v: lax.rem(v + 3, 4)
    op = lambda v: lax.rem(v + 2, 4)
    xp, xm, x2 = up(x), dn(x), op(x)
    yp, ym, y2 = up(y), dn(y), op(y)
    hp, hm, h2 = up(h), dn(h), op(h)
    col = lambda l_, y_, k_: (l_ * 4 + y_) * 2 + k_
    to_xp, to_xm = {"row": xp}, {"row": xm}
    to_hp, to_hm = {"depth": hp}, {"depth": hm}
    to_yp, to_ym = {"col": col(l, yp, k)}, {"col": col(l, ym, k)}
    to_core, to_pair = {"col": col(l, y, ok)}, {"col": col(ol, y, k)}
    plane = [to_hp, to_hm, {"depth": h2}, to_pair] + [
        {"depth": d, "col": col(ol, y, k)} for d in (hp, hm, h2)
    ]

    barrier = pltpu.get_barrier_semaphore()
    greeted = plane + [to_xp, to_xm, to_yp, to_ym, to_core]
    for dev in greeted:
        pl.semaphore_signal(barrier, inc=1, device_id=dev, device_id_type=pl.DeviceIdType.MESH)

    started = []

    def send(src, dst, dev):
        i = len(started)
        d = pltpu.make_async_remote_copy(
            src_ref=src, dst_ref=dst, send_sem=ssem.at[i], recv_sem=rsem.at[i],
            device_id=dev, device_id_type=pl.DeviceIdType.MESH,
        )
        d.start()
        started.append(d)
        return d

    locs = []

    def local(src, dst):
        d = pltpu.make_async_copy(src, dst, lsem.at[len(locs)])
        d.start()
        locs.append(d)
        return d

    HA, HB = pl.ds(0, 64), pl.ds(64, 64)
    cols_of = lambda d: pl.ds(pl.multiple_of(d * 768, 768), 768)

    l_og = local(og, OG.at[h, x])
    l_w = local(wt.at[:, :, k], W.at[:, :, :, pl.ds(0, 1152)])
    l_act = local(act.at[:, cols_of(h)], ACT.at[h, l, y, k])
    pl.semaphore_wait(barrier, len(greeted))

    mine = lambda half: og.at[half]
    d_core_og = [send(og, OGP.at[0], to_core)]
    x0a = send(mine(HA), OG.at[h, x, HA], to_xp)
    x0b = send(mine(HB), OG.at[h, x, HB], to_xm)
    z0a = send(mine(HA), OG.at[h, x, HA], to_hp)
    z0b = send(mine(HB), OG.at[h, x, HB], to_hm)
    d_w = send(wt.at[:, :, ok], W.at[:, :, :, pl.ds(1152, 1152)], to_core)
    x0c = send(mine(HB), OG.at[h, x, HB], to_xp)
    x0d = send(mine(HA), OG.at[h, x, HA], to_xm)
    d_act = []
    for dev in plane:
        d_act.append(send(act.at[:, cols_of(dev.get("depth", h))], ACT.at[h, l, y, k], dev))
    z0c = send(mine(HB), OG.at[h, x, HB], to_hp)
    z0d = send(mine(HA), OG.at[h, x, HA], to_hm)

    def fwd_x(H, first, second):
        first.wait_recv()
        f0 = send(OG.at[H, xm, HA], OG.at[H, xm, HA], to_xp)
        second.wait_recv()
        f1 = send(OG.at[H, xp, HB], OG.at[H, xp, HB], to_xm)
        return f0, f1

    order = [x, xm, xp, x2]

    def part(t):
        ogs = jnp.concatenate([OG[h, order[t]], OGP[t]], axis=1)

        @pl.loop(0, 2)
        def _(i):
            w = W[i].reshape(768, 2304)
            PT[t, i] = lax.dot_general(
                w, ogs, (((1,), (1,)), ((), ())), preferred_element_type=F32
            ).reshape(4, 192, 128)

    FA, FB = pl.ds(0, 96), pl.ds(96, 96)

    def rs_begin(t):
        part(t)
        return dict(
            p1=send(PT.at[t, :, y2, FA], R1.at[t, 0], to_yp),
            m1=send(PT.at[t, :, y2, FB], R1.at[t, 1], to_ym),
            p2=send(PT.at[t, :, yp, FB], R2.at[t, 0, :, FB], to_yp),
            m2=send(PT.at[t, :, ym, FA], R2.at[t, 1, :, FA], to_ym),
        )

    def rs_mid(t, s):
        s["p1"].wait_recv()
        PT[t, :, yp, FA] = PT[t, :, yp, FA] + R1[t, 0]
        s["p3"] = send(PT.at[t, :, yp, FA], R2.at[t, 0, :, FA], to_yp)
        s["m1"].wait_recv()
        PT[t, :, ym, FB] = PT[t, :, ym, FB] + R1[t, 1]
        s["m3"] = send(PT.at[t, :, ym, FB], R2.at[t, 1, :, FB], to_ym)

    def rs_end(t, s):
        for n in ("p2", "m2", "p3", "m3"):
            s[n].wait_recv()
        SZ[t] = PT[t, ol, y] + R2[t, 0, ol] + R2[t, 1, ol]
        s["z"] = send(SZ.at[t], RZ.at[t], to_pair)
        FN[t] = PT[t, l, y] + R2[t, 0, l] + R2[t, 1, l]

    def rs_out(t, s):
        s["z"].wait_recv()
        FN[t] = FN[t] + RZ[t]
        return local(FN.at[t], ig_out.at[order[t]])

    def wg(H, first, last):
        for m in range(3):
            rows = pl.ds(m * 256, 256)
            a = ACT[H, :, :, :, :, rows].reshape(512, 256)
            g = OG[H].reshape(512, 1152)
            d = lax.dot_general(a, g, (((0,), (0,)), ((), ())), preferred_element_type=F32)
            ACC[rows] = d if first else ACC[rows] + d
            if last:
                local(ACC.at[rows], wg_out.at[rows])

    l_og.wait()
    x0e, x0f = fwd_x(h, x0a, x0b)
    x0c.wait_recv()
    d_core_og.append(send(OG.at[h, xm], OGP.at[1], to_core))
    x0d.wait_recv()
    d_core_og.append(send(OG.at[h, xp], OGP.at[2], to_core))
    l_w.wait()
    d_w.wait_recv()
    d_core_og[0].wait_recv()
    s0 = rs_begin(0)

    z0a.wait_recv()
    a1 = send(OG.at[hm, x, HA], OG.at[hm, x, HA], to_xp)
    z2a = send(OG.at[hm, x, HA], OG.at[hm, x, HA], to_hp)
    a2 = send(OG.at[hm, x, HA], OG.at[hm, x, HA], to_xm)
    z0b.wait_recv()
    b1 = send(OG.at[hp, x, HB], OG.at[hp, x, HB], to_xm)
    z2b = send(OG.at[hp, x, HB], OG.at[hp, x, HB], to_hm)
    b2 = send(OG.at[hp, x, HB], OG.at[hp, x, HB], to_xp)

    for d in d_act:
        d.wait_recv()
    l_act.wait()
    y_p = send(ACT.at[:, :, y, k], ACT.at[:, :, y, k], to_yp)
    y_m = send(ACT.at[:, :, y, k], ACT.at[:, :, y, k], to_ym)
    c_act = [send(ACT.at[:, :, y, k], ACT.at[:, :, y, k], to_core)]

    x0e.wait_recv()
    x0f.wait_recv()
    d_core_og.append(send(OG.at[h, x2], OGP.at[3], to_core))
    d_core_og[1].wait_recv()
    s1 = rs_begin(1)
    rs_mid(0, s0)
    d_core_og[2].wait_recv()
    s2 = rs_begin(2)

    z0c.wait_recv()
    a3 = send(OG.at[hm, x, HB], OG.at[hm, x, HB], to_xm)
    a4 = send(OG.at[hm, x, HB], OG.at[hm, x, HB], to_xp)
    z0d.wait_recv()
    b3 = send(OG.at[hp, x, HA], OG.at[hp, x, HA], to_xp)
    b4 = send(OG.at[hp, x, HA], OG.at[hp, x, HA], to_xm)

    d_core_og[3].wait_recv()
    s3 = rs_begin(3)
    rs_mid(1, s1)
    rs_end(0, s0)
    a5, a6 = fwd_x(hm, a1, a3)
    b5, b6 = fwd_x(hp, b3, b1)

    y_p.wait_recv()
    y_fp = send(ACT.at[:, 0, ym, k], ACT.at[:, 0, ym, k], to_yp)
    c_act.append(send(ACT.at[:, :, ym, k], ACT.at[:, :, ym, k], to_core))
    y_m.wait_recv()
    y_fm = send(ACT.at[:, 1, yp, k], ACT.at[:, 1, yp, k], to_ym)
    c_act.append(send(ACT.at[:, :, yp, k], ACT.at[:, :, yp, k], to_core))

    z2a.wait_recv()
    e1 = send(OG.at[h2, x, HA], OG.at[h2, x, HA], to_xp)
    e2 = send(OG.at[h2, x, HA], OG.at[h2, x, HA], to_xm)
    z2b.wait_recv()
    e3 = send(OG.at[h2, x, HB], OG.at[h2, x, HB], to_xm)
    e4 = send(OG.at[h2, x, HB], OG.at[h2, x, HB], to_xp)

    rs_mid(2, s2)
    rs_mid(3, s3)
    rs_end(1, s1)
    y_fp.wait_recv()
    y_fm.wait_recv()
    c_act.append(send(ACT.at[:, :, y2, k], ACT.at[:, :, y2, k], to_core))
    rs_out(0, s0)
    e5, e6 = fwd_x(h2, e1, e3)
    rs_end(2, s2)
    rs_out(1, s1)
    for d in c_act:
        d.wait_recv()
    wg(h, True, False)
    for d in (a2, a4, a5, a6):
        d.wait_recv()
    for d in (b2, b4, b5, b6):
        d.wait_recv()
    rs_end(3, s3)
    rs_out(2, s2)
    wg(hm, False, False)
    wg(hp, False, False)
    rs_out(3, s3)
    for d in (e2, e4, e5, e6):
        d.wait_recv()
    wg(h2, False, True)
    for d in locs[3:]:
        d.wait()
    for d in started:
        d.wait_send()


def body(activations, out_grad, weight):
    any_ = pl.BlockSpec(memory_space=pl.ANY)
    ig, wg = pl.pallas_call(
        kernel,
        out_shape=(
            jax.ShapeDtypeStruct((4, 192, 128), F32),
            jax.ShapeDtypeStruct((768, 1152), F32),
        ),
        in_specs=[any_] * 3,
        out_specs=(any_, any_),
        scratch_shapes=[
            pltpu.VMEM((2, 4, 192, 2304), BF16),
            pltpu.VMEM((4, 4, 128, 1152), BF16),
            pltpu.VMEM((4, 128, 1152), BF16),
            pltpu.VMEM((4, 2, 4, 2, 32, 768), BF16),
            pltpu.VMEM((4, 2, 4, 192, 128), F32),
            pltpu.VMEM((4, 2, 2, 96, 128), F32),
            pltpu.VMEM((4, 2, 2, 192, 128), F32),
            pltpu.VMEM((4, 192, 128), F32),
            pltpu.VMEM((4, 192, 128), F32),
            pltpu.VMEM((4, 192, 128), F32),
            pltpu.VMEM((768, 1152), F32),
            pltpu.SemaphoreType.DMA((SEMS,)),
            pltpu.SemaphoreType.DMA((SEMS,)),
            pltpu.SemaphoreType.DMA((16,)),
        ],
        compiler_params=pltpu.CompilerParams(
            collective_id=0, has_side_effects=True, vmem_limit_bytes=56 * 1024 * 1024
        ),
        cost_estimate=pl.CostEstimate(flops=7_300_000_000, bytes_accessed=20_000_000, transcendentals=0),
    )(activations, out_grad, weight.reshape(2, 4, 2, 192, 1152))
    input_grad = jnp.transpose(ig, (0, 2, 1)).reshape(512, 192).astype(BF16)
    return input_grad, wg.reshape(1, 1, 768, 1152)


def solution(mesh):
    return jax.shard_map(
        body,
        mesh=mesh,
        in_specs=(P(("depth", "col"), "row"), P(("depth", "row"), "col"), P("row", "col")),
        out_specs=(P("depth", ("row", "col")), P("row", "depth", None, "col")),
        check_vma=False,
    )
```

```python
import jax
import jax.numpy as jnp
from jax import lax
from jax.experimental import pallas as pl
from jax.experimental.pallas import tpu as pltpu
from jax.sharding import PartitionSpec as P

F32 = jnp.float32
BF16 = jnp.bfloat16
SEMS = 64


def kernel(act, og, wt, ig_out, wg_out, W, OG, OGP, ACT, PT, R1, R2, SZ, RZ, FN, ACC, ssem, rsem, lsem):
    h = lax.axis_index("depth")
    x = lax.axis_index("row")
    c = lax.axis_index("col")
    k = lax.rem(c, 2)
    y = lax.rem(lax.div(c, 2), 4)
    l = lax.div(c, 8)
    ok, ol = 1 - k, 1 - l
    up = lambda v: lax.rem(v + 1, 4)
    dn = lambda v: lax.rem(v + 3, 4)
    op = lambda v: lax.rem(v + 2, 4)
    xp, xm, x2 = up(x), dn(x), op(x)
    yp, ym, y2 = up(y), dn(y), op(y)
    hp, hm, h2 = up(h), dn(h), op(h)
    col = lambda l_, y_, k_: (l_ * 4 + y_) * 2 + k_
    to_xp, to_xm = {"row": xp}, {"row": xm}
    to_hp, to_hm = {"depth": hp}, {"depth": hm}
    to_yp, to_ym = {"col": col(l, yp, k)}, {"col": col(l, ym, k)}
    to_core, to_pair = {"col": col(l, y, ok)}, {"col": col(ol, y, k)}
    plane = [to_hp, to_hm, {"depth": h2}, to_pair] + [
        {"depth": d, "col": col(ol, y, k)} for d in (hp, hm, h2)
    ]

    barrier = pltpu.get_barrier_semaphore()
    greeted = plane + [to_xp, to_xm, to_yp, to_ym, to_core]
    for dev in greeted:
        pl.semaphore_signal(barrier, inc=1, device_id=dev, device_id_type=pl.DeviceIdType.MESH)

    started = []
    used = [0]

    class Group:
        def __init__(self, whole):
            self.i = used[0]
            used[0] += 1
            self.d = pltpu.make_async_remote_copy(
                src_ref=whole, dst_ref=whole, send_sem=ssem.at[self.i], recv_sem=rsem.at[self.i],
                device_id=to_core, device_id_type=pl.DeviceIdType.MESH,
            )
            started.append(self.d)

        def send(self, src, dst, dev):
            pltpu.make_async_remote_copy(
                src_ref=src, dst_ref=dst, send_sem=ssem.at[self.i], recv_sem=rsem.at[self.i],
                device_id=dev, device_id_type=pl.DeviceIdType.MESH,
            ).start()

        def wait(self):
            self.d.wait_recv()

    def send(src, dst, dev):
        g = Group(dst)
        g.send(src, dst, dev)
        return g

    locs = []

    def local(src, dst):
        d = pltpu.make_async_copy(src, dst, lsem.at[len(locs)])
        d.start()
        locs.append(d)
        return d

    HA, HB = pl.ds(0, 64), pl.ds(64, 64)
    cols_of = lambda d: pl.ds(pl.multiple_of(d * 768, 768), 768)

    l_og = local(og, OG.at[h, x])
    l_w = local(wt.at[:, :, k], W.at[:, :, :, pl.ds(0, 1152)])
    l_act = local(act.at[:, cols_of(h)], ACT.at[h, l, y, k])
    pl.semaphore_wait(barrier, len(greeted))

    two_halves = OG.at[h, x]
    depths = [h, hm, hp, h2]

    x0a = send(og.at[HA], OG.at[h, x, HA], to_xp)
    x0b = send(og.at[HB], OG.at[h, x, HB], to_xm)
    z0ab, z0cd, z2ab = Group(two_halves), Group(two_halves), Group(two_halves)
    z0ab.send(og.at[HA], OG.at[h, x, HA], to_hp)
    z0ab.send(og.at[HB], OG.at[h, x, HB], to_hm)
    c_og0 = send(og, OGP.at[0], to_core)
    ring = [y2, yp, ym, y]
    to_other = lambda v: send(wt.at[:, v, ok], W.at[:, v, :, pl.ds(1152, 1152)], to_core)
    d_w = [to_other(v) for v in ring[:2]]
    x0cd, x0ef = Group(two_halves), Group(two_halves)
    x0cd.send(og.at[HB], OG.at[h, x, HB], to_xp)
    x0cd.send(og.at[HA], OG.at[h, x, HA], to_xm)
    y_pm = [Group(ACT.at[d, :, pl.ds(0, 2), k]) for d in depths]
    own_act = act.at[:, cols_of(h)]
    y_pm[0].send(own_act, ACT.at[h, l, y, k], to_yp)
    y_pm[0].send(own_act, ACT.at[h, l, y, k], to_ym)
    d_w += [to_other(v) for v in ring[2:]]
    z0cd.send(og.at[HB], OG.at[h, x, HB], to_hp)
    z0cd.send(og.at[HA], OG.at[h, x, HA], to_hm)
    d_act = []
    for dev in plane:
        d_act.append(send(act.at[:, cols_of(dev.get("depth", h))], ACT.at[h, l, y, k], dev))

    order = [x, xm, xp, x2]
    FA, FB = pl.ds(0, 96), pl.ds(96, 96)

    class Terms:
        def __init__(self, t, n):
            self.t, self.n, self.at = t, n, pl.ds(t, n)
            self.g1, self.g2 = Group(R1.at[self.at]), Group(R2.at[self.at])

        def load(self):
            own = [OG[h, order[t]] for t in range(self.t, self.t + self.n)]
            other = [OGP[t] for t in range(self.t, self.t + self.n)]
            self.ogs = jnp.concatenate(
                [jnp.concatenate(own, axis=0), jnp.concatenate(other, axis=0)], axis=1
            )

        def part(self, i):
            v = ring[i]
            r = lax.dot_general(
                W[:, v].reshape(384, 2304), self.ogs, (((1,), (1,)), ((), ())),
                preferred_element_type=F32,
            )
            for j in range(self.n):
                PT[self.t + j, :, v] = r[:, j * 128 : (j + 1) * 128].reshape(2, 192, 128)

        def far(self):
            self.part(0)
            self.g1.send(PT.at[self.at, :, y2, FA], R1.at[self.at, 0], to_yp)
            self.g1.send(PT.at[self.at, :, y2, FB], R1.at[self.at, 1], to_ym)

        def near_p(self):
            self.part(1)
            self.g2.send(PT.at[self.at, :, yp, FB], R2.at[self.at, 0, :, FB], to_yp)

        def near_m(self):
            self.part(2)
            self.g2.send(PT.at[self.at, :, ym, FA], R2.at[self.at, 1, :, FA], to_ym)

        def all(self):
            self.load()
            self.far()
            self.near_p()
            self.near_m()
            self.part(3)

        def mid(self):
            self.g1.wait()
            for t in range(self.t, self.t + self.n):
                PT[t, :, yp, FA] = PT[t, :, yp, FA] + R1[t, 0]
                PT[t, :, ym, FB] = PT[t, :, ym, FB] + R1[t, 1]
            self.g2.send(PT.at[self.at, :, yp, FA], R2.at[self.at, 0, :, FA], to_yp)
            self.g2.send(PT.at[self.at, :, ym, FB], R2.at[self.at, 1, :, FB], to_ym)

        def end(self):
            self.g2.wait()
            for t in range(self.t, self.t + self.n):
                SZ[t] = PT[t, ol, y] + R2[t, 0, ol] + R2[t, 1, ol]
            self.z = send(SZ.at[self.at], RZ.at[self.at], to_pair)
            for t in range(self.t, self.t + self.n):
                FN[t] = PT[t, l, y] + R2[t, 0, l] + R2[t, 1, l]

        def out(self):
            self.z.wait()
            for t in range(self.t, self.t + self.n):
                FN[t] = FN[t] + RZ[t]
                local(FN.at[t], ig_out.at[order[t]])

    def wg(H, first, last):
        for m in range(3):
            rows = pl.ds(m * 256, 256)
            a = ACT[H, :, :, :, :, rows].reshape(512, 256)
            g = OG[H].reshape(512, 1152)
            d = lax.dot_general(a, g, (((0,), (0,)), ((), ())), preferred_element_type=F32)
            ACC[rows] = d if first else ACC[rows] + d
            if last:
                local(ACC.at[rows], wg_out.at[rows])

    def again(group, H, X, half, dev):
        group.send(OG.at[H, X, half], OG.at[H, X, half], dev)

    s0, s1, s3 = Terms(0, 1), Terms(1, 2), Terms(3, 1)
    l_og.wait()
    l_w.wait()
    c_og0.wait()
    s0.load()
    d_w[0].wait()
    s0.far()
    d_w[1].wait()
    s0.near_p()
    x0a.wait()
    again(x0ef, h, xm, HA, to_xp)
    x0b.wait()
    again(x0ef, h, xp, HB, to_xm)
    d_w[2].wait()
    s0.near_m()
    d_w[3].wait()
    s0.part(3)
    s0.mid()
    c_og12 = Group(OGP.at[pl.ds(1, 2)])
    x0cd.wait()
    c_og12.send(OG.at[h, xm], OGP.at[1], to_core)
    c_og12.send(OG.at[h, xp], OGP.at[2], to_core)

    ab1, ab3 = Group(two_halves), Group(two_halves)
    a_in, b_in = Group(OG.at[h, pl.ds(0, 2)]), Group(OG.at[h, pl.ds(0, 2)])
    z0ab.wait()
    again(ab1, hm, x, HA, to_xp)
    again(ab1, hp, x, HB, to_xm)
    again(a_in, hm, x, HA, to_xm)
    again(b_in, hp, x, HB, to_xp)
    again(z2ab, hm, x, HA, to_hp)
    again(z2ab, hp, x, HB, to_hm)

    c_og12.wait()
    s1.all()
    x0ef.wait()
    c_og3 = send(OG.at[h, x2], OGP.at[3], to_core)
    s0.end()
    c_og3.wait()
    s3.all()
    ab1.wait()
    again(a_in, hm, xm, HA, to_xp)
    again(b_in, hp, xp, HB, to_xm)
    s1.mid()
    z0cd.wait()
    again(ab3, hm, x, HB, to_xm)
    again(ab3, hp, x, HA, to_xp)
    again(a_in, hm, x, HB, to_xp)
    again(b_in, hp, x, HA, to_xm)
    s3.mid()

    def act_y(i):
        d = depths[i]
        own = ACT.at[d, ol, y, k] if i == 0 else ACT.at[d, :, y, k]
        y_pm[i].send(own, own, to_yp)
        y_pm[i].send(own, own, to_ym)

    y_f = [Group(ACT.at[d, :, 0, k]) for d in depths]
    c_act = [Group(ACT.at[d, :, pl.ds(0, 3), k]) for d in depths]

    def act_in(i):
        d = depths[i]
        y_pm[i].wait()
        y_f[i].send(ACT.at[d, 0, ym, k], ACT.at[d, 0, ym, k], to_yp)
        y_f[i].send(ACT.at[d, 1, yp, k], ACT.at[d, 1, yp, k], to_ym)
        for v in (ym, yp):
            c_act[i].send(ACT.at[d, :, v, k], ACT.at[d, :, v, k], to_core)

    def act_all(i):
        d = depths[i]
        y_f[i].wait()
        c_act[i].send(ACT.at[d, :, y2, k], ACT.at[d, :, y2, k], to_core)

    for d in d_act:
        d.wait()
    l_act.wait()
    act_y(0)
    act_y(1)
    c_own = send(ACT.at[:, :, y, k], ACT.at[:, :, y, k], to_core)
    ab3.wait()
    again(b_in, hp, xm, HA, to_xp)
    again(a_in, hm, xp, HB, to_xm)
    s0.out()
    s1.end()
    e13, e_in = Group(two_halves), Group(OG.at[h, pl.ds(0, 2)])
    z2ab.wait()
    again(e13, h2, x, HA, to_xp)
    again(e13, h2, x, HB, to_xm)
    again(e_in, h2, x, HA, to_xm)
    again(e_in, h2, x, HB, to_xp)
    s3.end()
    act_in(0)
    act_y(2)
    s1.out()
    act_in(1)
    act_y(3)
    act_all(0)
    s3.out()
    e13.wait()
    again(e_in, h2, xm, HA, to_xp)
    again(e_in, h2, xp, HB, to_xm)
    c_own.wait()
    c_act[0].wait()
    wg(h, True, False)
    act_in(2)
    act_all(1)
    a_in.wait()
    c_act[1].wait()
    wg(hm, False, False)
    act_in(3)
    act_all(2)
    b_in.wait()
    c_act[2].wait()
    wg(hp, False, False)
    act_all(3)
    e_in.wait()
    c_act[3].wait()
    wg(h2, False, True)
    for d in locs[3:]:
        d.wait()
    for d in started:
        d.wait_send()


def body(activations, out_grad, weight):
    any_ = pl.BlockSpec(memory_space=pl.ANY)
    ig, wg = pl.pallas_call(
        kernel,
        out_shape=(
            jax.ShapeDtypeStruct((4, 192, 128), F32),
            jax.ShapeDtypeStruct((768, 1152), F32),
        ),
        in_specs=[any_] * 3,
        out_specs=(any_, any_),
        scratch_shapes=[
            pltpu.VMEM((2, 4, 192, 2304), BF16),
            pltpu.VMEM((4, 4, 128, 1152), BF16),
            pltpu.VMEM((4, 128, 1152), BF16),
            pltpu.VMEM((4, 2, 4, 2, 32, 768), BF16),
            pltpu.VMEM((4, 2, 4, 192, 128), F32),
            pltpu.VMEM((4, 2, 2, 96, 128), F32),
            pltpu.VMEM((4, 2, 2, 192, 128), F32),
            pltpu.VMEM((4, 192, 128), F32),
            pltpu.VMEM((4, 192, 128), F32),
            pltpu.VMEM((4, 192, 128), F32),
            pltpu.VMEM((768, 1152), F32),
            pltpu.SemaphoreType.DMA((SEMS,)),
            pltpu.SemaphoreType.DMA((SEMS,)),
            pltpu.SemaphoreType.DMA((16,)),
        ],
        compiler_params=pltpu.CompilerParams(
            collective_id=0, has_side_effects=True, vmem_limit_bytes=56 * 1024 * 1024
        ),
        cost_estimate=pl.CostEstimate(flops=7_300_000_000, bytes_accessed=20_000_000, transcendentals=0),
    )(activations, out_grad, weight.reshape(2, 4, 2, 192, 1152))
    input_grad = jnp.transpose(ig, (0, 2, 1)).reshape(512, 192).astype(BF16)
    return input_grad, wg.reshape(1, 1, 768, 1152)


def solution(mesh):
    return jax.shard_map(
        body,
        mesh=mesh,
        in_specs=(P(("depth", "col"), "row"), P(("depth", "row"), "col"), P("row", "col")),
        out_specs=(P("depth", ("row", "col")), P("row", "depth", None, "col")),
        check_vma=False,
    )
```

```python
import jax
import jax.numpy as jnp
from jax import lax
from jax.experimental import pallas as pl
from jax.experimental.pallas import tpu as pltpu
from jax.sharding import PartitionSpec as P

F32 = jnp.float32
BF16 = jnp.bfloat16
SEMS = 64


def kernel(act, og, wt, ig_out, ACC, W, OG, OGP, ACT, PT, R1, R2, SZ, RZ, FN, ssem, rsem, lsem):
    h = lax.axis_index("depth")
    x = lax.axis_index("row")
    c = lax.axis_index("col")
    k = lax.rem(c, 2)
    y = lax.rem(lax.div(c, 2), 4)
    l = lax.div(c, 8)
    ok, ol = 1 - k, 1 - l
    up = lambda v: lax.rem(v + 1, 4)
    dn = lambda v: lax.rem(v + 3, 4)
    op = lambda v: lax.rem(v + 2, 4)
    xp, xm, x2 = up(x), dn(x), op(x)
    yp, ym, y2 = up(y), dn(y), op(y)
    hp, hm, h2 = up(h), dn(h), op(h)
    col = lambda l_, y_, k_: (l_ * 4 + y_) * 2 + k_
    to_xp, to_xm = {"row": xp}, {"row": xm}
    to_hp, to_hm = {"depth": hp}, {"depth": hm}
    to_yp, to_ym = {"col": col(l, yp, k)}, {"col": col(l, ym, k)}
    to_core, to_pair = {"col": col(l, y, ok)}, {"col": col(ol, y, k)}
    plane = [to_hp, to_hm, {"depth": h2}, to_pair] + [
        {"depth": d, "col": col(ol, y, k)} for d in (hp, hm, h2)
    ]

    barrier = pltpu.get_barrier_semaphore()
    greeted = plane + [to_xp, to_xm, to_yp, to_ym, to_core]
    for dev in greeted:
        pl.semaphore_signal(barrier, inc=1, device_id=dev, device_id_type=pl.DeviceIdType.MESH)

    started = []
    used = [0]

    class Group:
        def __init__(self, whole):
            self.i = used[0]
            used[0] += 1
            self.d = pltpu.make_async_remote_copy(
                src_ref=whole, dst_ref=whole, send_sem=ssem.at[self.i], recv_sem=rsem.at[self.i],
                device_id=to_core, device_id_type=pl.DeviceIdType.MESH,
            )
            started.append(self.d)

        def send(self, src, dst, dev):
            pltpu.make_async_remote_copy(
                src_ref=src, dst_ref=dst, send_sem=ssem.at[self.i], recv_sem=rsem.at[self.i],
                device_id=dev, device_id_type=pl.DeviceIdType.MESH,
            ).start()

        def wait(self):
            self.d.wait_recv()

    def send(src, dst, dev):
        g = Group(dst)
        g.send(src, dst, dev)
        return g

    locs = []

    def local(src, dst):
        d = pltpu.make_async_copy(src, dst, lsem.at[len(locs)])
        d.start()
        locs.append(d)
        return d

    HA, HB = pl.ds(0, 64), pl.ds(64, 64)
    cols_of = lambda d: pl.ds(pl.multiple_of(d * 768, 768), 768)

    l_og = local(og, OG.at[h, x])
    l_w = local(wt.at[:, :, k], W.at[:, :, :, pl.ds(0, 1152)])
    l_act = local(act.at[:, cols_of(h)], ACT.at[h, l, y, k])
    pl.semaphore_wait(barrier, len(greeted))

    two_halves = OG.at[h, x]
    depths = [h, hm, hp, h2]

    x0a = send(og.at[HA], OG.at[h, x, HA], to_xp)
    x0b = send(og.at[HB], OG.at[h, x, HB], to_xm)
    z0ab, z0cd, z2ab = Group(two_halves), Group(two_halves), Group(two_halves)
    z0ab.send(og.at[HA], OG.at[h, x, HA], to_hp)
    z0ab.send(og.at[HB], OG.at[h, x, HB], to_hm)
    c_og0 = send(og, OGP.at[0], to_core)
    ring = [y2, yp, ym, y]
    to_other = lambda v: send(wt.at[:, v, ok], W.at[:, v, :, pl.ds(1152, 1152)], to_core)
    d_w = [to_other(v) for v in ring[:2]]
    x0cd, x0ef = Group(two_halves), Group(two_halves)
    x0cd.send(og.at[HB], OG.at[h, x, HB], to_xp)
    x0cd.send(og.at[HA], OG.at[h, x, HA], to_xm)
    y_pm = [Group(ACT.at[d, :, pl.ds(0, 2), k]) for d in depths]
    own_act = act.at[:, cols_of(h)]
    y_pm[0].send(own_act, ACT.at[h, l, y, k], to_yp)
    y_pm[0].send(own_act, ACT.at[h, l, y, k], to_ym)
    d_w += [to_other(v) for v in ring[2:]]
    z0cd.send(og.at[HB], OG.at[h, x, HB], to_hp)
    z0cd.send(og.at[HA], OG.at[h, x, HA], to_hm)
    d_act = []
    for dev in plane:
        d_act.append(send(act.at[:, cols_of(dev.get("depth", h))], ACT.at[h, l, y, k], dev))

    order = [x, xm, xp, x2]
    FA, FB = pl.ds(0, 96), pl.ds(96, 96)

    class Terms:
        def __init__(self, t, n):
            self.t, self.n, self.at = t, n, pl.ds(t, n)
            self.g1, self.g2 = Group(R1.at[self.at]), Group(R2.at[self.at])

        def load(self):
            own = [OG[h, order[t]] for t in range(self.t, self.t + self.n)]
            other = [OGP[t] for t in range(self.t, self.t + self.n)]
            self.ogs = jnp.concatenate(
                [jnp.concatenate(own, axis=0), jnp.concatenate(other, axis=0)], axis=1
            )

        def part(self, i):
            v = ring[i]
            r = lax.dot_general(
                W[:, v].reshape(384, 2304), self.ogs, (((1,), (1,)), ((), ())),
                preferred_element_type=F32,
            )
            for j in range(self.n):
                PT[self.t + j, :, v] = r[:, j * 128 : (j + 1) * 128].reshape(2, 192, 128)

        def far(self):
            self.g1.send(PT.at[self.at, :, y2, FA], R1.at[self.at, 0], to_yp)
            self.g1.send(PT.at[self.at, :, y2, FB], R1.at[self.at, 1], to_ym)

        def near(self):
            self.g2.send(PT.at[self.at, :, yp, FB], R2.at[self.at, 0, :, FB], to_yp)
            self.g2.send(PT.at[self.at, :, ym, FA], R2.at[self.at, 1, :, FA], to_ym)

        def all(self):
            self.load()
            r = lax.dot_general(
                W[...].reshape(1536, 2304), self.ogs, (((1,), (1,)), ((), ())),
                preferred_element_type=F32,
            )
            for j in range(self.n):
                PT[self.t + j] = r[:, j * 128 : (j + 1) * 128].reshape(2, 4, 192, 128)
            self.far()
            self.near()

        def mid(self):
            self.g1.wait()
            for t in range(self.t, self.t + self.n):
                PT[t, :, yp, FA] = PT[t, :, yp, FA] + R1[t, 0]
                PT[t, :, ym, FB] = PT[t, :, ym, FB] + R1[t, 1]
            self.g2.send(PT.at[self.at, :, yp, FA], R2.at[self.at, 0, :, FA], to_yp)
            self.g2.send(PT.at[self.at, :, ym, FB], R2.at[self.at, 1, :, FB], to_ym)

        def end(self):
            self.g2.wait()
            for t in range(self.t, self.t + self.n):
                SZ[t] = PT[t, ol, y] + R2[t, 0, ol] + R2[t, 1, ol]
            self.z = send(SZ.at[self.at], RZ.at[self.at], to_pair)
            for t in range(self.t, self.t + self.n):
                FN[t] = PT[t, l, y] + R2[t, 0, l] + R2[t, 1, l]

        def out(self):
            self.z.wait()
            for t in range(self.t, self.t + self.n):
                at = pl.ds(pl.multiple_of(order[t] * 128, 128), 128)
                ig_out[:, at] = (FN[t] + RZ[t]).astype(BF16)

    def wg(H, first):
        for m in range(3):
            rows = pl.ds(m * 256, 256)
            a = ACT[H, :, :, :, :, rows].reshape(512, 256)
            g = OG[H].reshape(512, 1152)
            d = lax.dot_general(a, g, (((0,), (0,)), ((), ())), preferred_element_type=F32)
            ACC[rows] = d if first else ACC[rows] + d

    def again(group, H, X, half, dev):
        group.send(OG.at[H, X, half], OG.at[H, X, half], dev)

    s0, s1, s3 = Terms(0, 1), Terms(1, 2), Terms(3, 1)
    l_og.wait()
    l_w.wait()
    c_og0.wait()
    s0.load()
    d_w[0].wait()
    s0.part(0)
    s0.far()
    x0a.wait()
    again(x0ef, h, xm, HA, to_xp)
    d_w[1].wait()
    d_w[2].wait()
    s0.part(1)
    s0.part(2)
    s0.near()
    x0b.wait()
    again(x0ef, h, xp, HB, to_xm)
    s0.mid()

    c_og12 = Group(OGP.at[pl.ds(1, 2)])
    x0cd.wait()
    c_og12.send(OG.at[h, xm], OGP.at[1], to_core)
    c_og12.send(OG.at[h, xp], OGP.at[2], to_core)

    ab1, ab3 = Group(two_halves), Group(two_halves)
    a_in, b_in = Group(OG.at[h, pl.ds(0, 2)]), Group(OG.at[h, pl.ds(0, 2)])
    z0ab.wait()
    again(ab1, hm, x, HA, to_xp)
    again(ab1, hp, x, HB, to_xm)
    again(a_in, hm, x, HA, to_xm)
    again(b_in, hp, x, HB, to_xp)
    again(z2ab, hm, x, HA, to_hp)
    again(z2ab, hp, x, HB, to_hm)
    d_w[3].wait()
    s0.part(3)

    c_og12.wait()
    s1.load()
    s1.part(0)
    s1.far()
    s1.part(1)
    s1.part(2)
    s1.near()
    x0ef.wait()
    c_og3 = send(OG.at[h, x2], OGP.at[3], to_core)
    s1.part(3)
    ab1.wait()
    again(a_in, hm, xm, HA, to_xp)
    again(b_in, hp, xp, HB, to_xm)
    z0cd.wait()
    again(ab3, hm, x, HB, to_xm)
    again(ab3, hp, x, HA, to_xp)
    again(a_in, hm, x, HB, to_xp)
    again(b_in, hp, x, HA, to_xm)
    s0.end()
    c_og3.wait()
    s3.all()
    s1.mid()
    s3.mid()

    def act_y(i):
        d = depths[i]
        own = ACT.at[d, ol, y, k] if i == 0 else ACT.at[d, :, y, k]
        y_pm[i].send(own, own, to_yp)
        y_pm[i].send(own, own, to_ym)

    y_f = [Group(ACT.at[d, :, 0, k]) for d in depths]
    c_act = [Group(ACT.at[d, :, pl.ds(0, 3), k]) for d in depths]

    def act_in(i):
        d = depths[i]
        y_pm[i].wait()
        y_f[i].send(ACT.at[d, 0, ym, k], ACT.at[d, 0, ym, k], to_yp)
        y_f[i].send(ACT.at[d, 1, yp, k], ACT.at[d, 1, yp, k], to_ym)
        for v in (ym, yp):
            c_act[i].send(ACT.at[d, :, v, k], ACT.at[d, :, v, k], to_core)

    def act_all(i):
        d = depths[i]
        y_f[i].wait()
        c_act[i].send(ACT.at[d, :, y2, k], ACT.at[d, :, y2, k], to_core)

    for d in d_act:
        d.wait()
    l_act.wait()
    act_y(0)
    act_y(1)
    act_y(2)
    c_own = send(ACT.at[:, :, y, k], ACT.at[:, :, y, k], to_core)
    ab3.wait()
    again(b_in, hp, xm, HA, to_xp)
    again(a_in, hm, xp, HB, to_xm)
    s0.out()
    s1.end()
    act_in(0)
    e13, e_in = Group(two_halves), Group(OG.at[h, pl.ds(0, 2)])
    z2ab.wait()
    again(e13, h2, x, HA, to_xp)
    again(e13, h2, x, HB, to_xm)
    again(e_in, h2, x, HA, to_xm)
    again(e_in, h2, x, HB, to_xp)
    s3.end()
    act_in(1)
    act_y(3)
    s1.out()
    act_in(2)
    act_all(0)
    e13.wait()
    again(e_in, h2, xm, HA, to_xp)
    again(e_in, h2, xp, HB, to_xm)
    c_own.wait()
    c_act[0].wait()
    wg(h, True)
    act_all(1)
    act_in(3)
    s3.out()
    a_in.wait()
    c_act[1].wait()
    wg(hm, False)
    act_all(2)
    b_in.wait()
    c_act[2].wait()
    act_all(3)
    wg(hp, False)
    e_in.wait()
    c_act[3].wait()
    wg(h2, False)
    for d in started:
        d.wait_send()


def body(activations, out_grad, weight):
    hbm = pl.BlockSpec(memory_space=pltpu.HBM)
    vmem = pl.BlockSpec(memory_space=pltpu.VMEM)
    input_grad, weight_grad = pl.pallas_call(
        kernel,
        out_shape=(pltpu.VMEM((192, 512), BF16), pltpu.VMEM((768, 1152), F32)),
        in_specs=[hbm] * 3,
        out_specs=(vmem, vmem),
        scratch_shapes=[
            pltpu.VMEM((2, 4, 192, 2304), BF16),
            pltpu.VMEM((4, 4, 128, 1152), BF16),
            pltpu.VMEM((4, 128, 1152), BF16),
            pltpu.VMEM((4, 2, 4, 2, 32, 768), BF16),
            pltpu.VMEM((4, 2, 4, 192, 128), F32),
            pltpu.VMEM((4, 2, 2, 96, 128), F32),
            pltpu.VMEM((4, 2, 2, 192, 128), F32),
            pltpu.VMEM((4, 192, 128), F32),
            pltpu.VMEM((4, 192, 128), F32),
            pltpu.VMEM((4, 192, 128), F32),
            pltpu.SemaphoreType.DMA((SEMS,)),
            pltpu.SemaphoreType.DMA((SEMS,)),
            pltpu.SemaphoreType.DMA((4,)),
        ],
        compiler_params=pltpu.CompilerParams(
            collective_id=0, has_side_effects=True, vmem_limit_bytes=48 * 1024 * 1024
        ),
        cost_estimate=pl.CostEstimate(flops=7_300_000_000, bytes_accessed=20_000_000, transcendentals=0),
    )(*[pltpu.with_memory_space_constraint(v, pltpu.HBM) for v in (activations, out_grad, weight.reshape(2, 4, 2, 192, 1152))])
    return input_grad.T, weight_grad.reshape(1, 1, 768, 1152)


def solution(mesh):
    return jax.shard_map(
        body,
        mesh=mesh,
        in_specs=(P(("depth", "col"), "row"), P(("depth", "row"), "col"), P("row", "col")),
        out_specs=(P("depth", ("row", "col")), P("row", "depth", None, "col")),
        check_vma=False,
    )
```

```python
import jax
import jax.numpy as jnp
from jax import lax
from jax.experimental import pallas as pl
from jax.experimental.pallas import tpu as pltpu
from jax.sharding import PartitionSpec as P

F32 = jnp.float32
BF16 = jnp.bfloat16
SEMS = 64


def kernel(act, og, wt, ig_out, ACC, W, OG, OGP, ACT, PT, R1, R2, SZ, RZ, FN, ssem, rsem, lsem):
    h = lax.axis_index("depth")
    x = lax.axis_index("row")
    c = lax.axis_index("col")
    k = lax.rem(c, 2)
    y = lax.rem(lax.div(c, 2), 4)
    l = lax.div(c, 8)
    ok, ol = 1 - k, 1 - l
    up = lambda v: lax.rem(v + 1, 4)
    dn = lambda v: lax.rem(v + 3, 4)
    op = lambda v: lax.rem(v + 2, 4)
    xp, xm, x2 = up(x), dn(x), op(x)
    yp, ym, y2 = up(y), dn(y), op(y)
    hp, hm, h2 = up(h), dn(h), op(h)
    col = lambda l_, y_, k_: (l_ * 4 + y_) * 2 + k_
    to_xp, to_xm = {"row": xp}, {"row": xm}
    to_hp, to_hm = {"depth": hp}, {"depth": hm}
    to_yp, to_ym = {"col": col(l, yp, k)}, {"col": col(l, ym, k)}
    to_core, to_pair = {"col": col(l, y, ok)}, {"col": col(ol, y, k)}
    plane = [to_hp, to_hm, {"depth": h2}, to_pair] + [
        {"depth": d, "col": col(ol, y, k)} for d in (hp, hm, h2)
    ]

    barrier = pltpu.get_barrier_semaphore()
    greeted = plane + [to_xp, to_xm, to_yp, to_ym, to_core]
    for dev in greeted:
        pl.semaphore_signal(barrier, inc=1, device_id=dev, device_id_type=pl.DeviceIdType.MESH)

    started = []
    used = [0]

    class Group:
        def __init__(self, whole):
            self.i = used[0]
            used[0] += 1
            self.d = pltpu.make_async_remote_copy(
                src_ref=whole, dst_ref=whole, send_sem=ssem.at[self.i], recv_sem=rsem.at[self.i],
                device_id=to_core, device_id_type=pl.DeviceIdType.MESH,
            )
            started.append(self.d)

        def send(self, src, dst, dev):
            pltpu.make_async_remote_copy(
                src_ref=src, dst_ref=dst, send_sem=ssem.at[self.i], recv_sem=rsem.at[self.i],
                device_id=dev, device_id_type=pl.DeviceIdType.MESH,
            ).start()

        def wait(self):
            self.d.wait_recv()

    def send(src, dst, dev):
        g = Group(dst)
        g.send(src, dst, dev)
        return g

    locs = []

    def local(src, dst):
        d = pltpu.make_async_copy(src, dst, lsem.at[len(locs)])
        d.start()
        locs.append(d)
        return d

    HA, HB = pl.ds(0, 64), pl.ds(64, 64)
    cols_of = lambda d: pl.ds(pl.multiple_of(d * 768, 768), 768)

    l_og = local(og, OG.at[h, x])
    l_w = local(wt.at[:, :, k], W.at[:, :, :, pl.ds(0, 1152)])
    l_act = local(act.at[:, cols_of(h)], ACT.at[h, l, y, k])
    pl.semaphore_wait(barrier, len(greeted))

    two_halves = OG.at[h, x]
    depths = [h, hm, hp, h2]

    x0a = send(og.at[HA], OG.at[h, x, HA], to_xp)
    x0b = send(og.at[HB], OG.at[h, x, HB], to_xm)
    z0ab, z0cd, z2ab = Group(two_halves), Group(two_halves), Group(two_halves)
    z0ab.send(og.at[HA], OG.at[h, x, HA], to_hp)
    z0ab.send(og.at[HB], OG.at[h, x, HB], to_hm)
    c_og0 = send(og, OGP.at[0], to_core)
    ring = [y2, yp, ym, y]
    to_other = lambda v: send(wt.at[:, v, ok], W.at[:, v, :, pl.ds(1152, 1152)], to_core)
    d_w = [to_other(v) for v in ring[:2]]
    x0cd, x0ef = Group(two_halves), Group(two_halves)
    x0cd.send(og.at[HB], OG.at[h, x, HB], to_xp)
    x0cd.send(og.at[HA], OG.at[h, x, HA], to_xm)
    y_pm = [Group(ACT.at[d, :, pl.ds(0, 2), k]) for d in depths]
    own_act = act.at[:, cols_of(h)]
    y_pm[0].send(own_act, ACT.at[h, l, y, k], to_yp)
    y_pm[0].send(own_act, ACT.at[h, l, y, k], to_ym)
    d_w += [to_other(v) for v in ring[2:]]
    z0cd.send(og.at[HB], OG.at[h, x, HB], to_hp)
    z0cd.send(og.at[HA], OG.at[h, x, HA], to_hm)
    d_act = []
    for dev in plane:
        d_act.append(send(act.at[:, cols_of(dev.get("depth", h))], ACT.at[h, l, y, k], dev))

    order = [x, xm, xp, x2]
    FA, FB = pl.ds(0, 96), pl.ds(96, 96)

    class Terms:
        def __init__(self, t, n):
            self.t, self.n, self.at = t, n, pl.ds(t, n)
            self.g1, self.g2 = Group(R1.at[self.at]), Group(R2.at[self.at])

        def load(self):
            own = [OG[h, order[t]] for t in range(self.t, self.t + self.n)]
            other = [OGP[t] for t in range(self.t, self.t + self.n)]
            self.ogs = jnp.concatenate(
                [jnp.concatenate(own, axis=0), jnp.concatenate(other, axis=0)], axis=1
            )

        def part(self, i):
            v = ring[i]
            r = lax.dot_general(
                W[:, v].reshape(384, 2304), self.ogs, (((1,), (1,)), ((), ())),
                preferred_element_type=F32,
            )
            for j in range(self.n):
                PT[self.t + j, :, v] = r[:, j * 128 : (j + 1) * 128].reshape(2, 192, 128)

        def far(self):
            self.g1.send(PT.at[self.at, :, y2, FA], R1.at[self.at, 0], to_yp)
            self.g1.send(PT.at[self.at, :, y2, FB], R1.at[self.at, 1], to_ym)

        def near(self):
            self.g2.send(PT.at[self.at, :, yp, FB], R2.at[self.at, 0, :, FB], to_yp)
            self.g2.send(PT.at[self.at, :, ym, FA], R2.at[self.at, 1, :, FA], to_ym)

        def all(self):
            self.load()
            r = lax.dot_general(
                W[...].reshape(1536, 2304), self.ogs, (((1,), (1,)), ((), ())),
                preferred_element_type=F32,
            )
            for j in range(self.n):
                PT[self.t + j] = r[:, j * 128 : (j + 1) * 128].reshape(2, 4, 192, 128)
            self.far()
            self.near()

        def mid(self):
            self.g1.wait()
            for t in range(self.t, self.t + self.n):
                PT[t, :, yp, FA] = PT[t, :, yp, FA] + R1[t, 0]
                PT[t, :, ym, FB] = PT[t, :, ym, FB] + R1[t, 1]
            self.g2.send(PT.at[self.at, :, yp, FA], R2.at[self.at, 0, :, FA], to_yp)
            self.g2.send(PT.at[self.at, :, ym, FB], R2.at[self.at, 1, :, FB], to_ym)

        def end(self):
            self.g2.wait()
            for t in range(self.t, self.t + self.n):
                SZ[t] = PT[t, ol, y] + R2[t, 0, ol] + R2[t, 1, ol]
            self.z = send(SZ.at[self.at], RZ.at[self.at], to_pair)
            for t in range(self.t, self.t + self.n):
                FN[t] = PT[t, l, y] + R2[t, 0, l] + R2[t, 1, l]

        def out(self):
            self.z.wait()
            for t in range(self.t, self.t + self.n):
                at = pl.ds(pl.multiple_of(order[t] * 128, 128), 128)
                ig_out[:, at] = (FN[t] + RZ[t]).astype(BF16)

    def wg(H, first):
        for m in range(3):
            rows = pl.ds(m * 256, 256)
            a = ACT[H, :, :, :, :, rows].reshape(512, 256)
            g = OG[H].reshape(512, 1152)
            d = lax.dot_general(a, g, (((0,), (0,)), ((), ())), preferred_element_type=F32)
            ACC[rows] = d if first else ACC[rows] + d

    def again(group, H, X, half, dev):
        group.send(OG.at[H, X, half], OG.at[H, X, half], dev)

    s0, s1, s3 = Terms(0, 1), Terms(1, 2), Terms(3, 1)
    l_og.wait()
    l_w.wait()
    c_og0.wait()
    s0.load()
    d_w[0].wait()
    s0.part(0)
    s0.far()
    x0a.wait()
    again(x0ef, h, xm, HA, to_xp)
    d_w[1].wait()
    d_w[2].wait()
    s0.part(1)
    s0.part(2)
    s0.near()
    x0b.wait()
    again(x0ef, h, xp, HB, to_xm)
    c_og12 = Group(OGP.at[pl.ds(1, 2)])
    x0cd.wait()
    c_og12.send(OG.at[h, xm], OGP.at[1], to_core)
    c_og12.send(OG.at[h, xp], OGP.at[2], to_core)
    s0.mid()
    c_og12.wait()
    s1.load()
    s1.part(0)
    s1.far()

    ab1, ab3 = Group(two_halves), Group(two_halves)
    a_in, b_in = Group(OG.at[h, pl.ds(0, 2)]), Group(OG.at[h, pl.ds(0, 2)])
    z0ab.wait()
    again(ab1, hm, x, HA, to_xp)
    again(ab1, hp, x, HB, to_xm)
    again(a_in, hm, x, HA, to_xm)
    again(b_in, hp, x, HB, to_xp)
    again(z2ab, hm, x, HA, to_hp)
    again(z2ab, hp, x, HB, to_hm)
    s1.part(1)
    s1.part(2)
    s1.near()
    x0ef.wait()
    c_og3 = send(OG.at[h, x2], OGP.at[3], to_core)
    d_w[3].wait()
    s0.part(3)
    s1.part(3)
    ab1.wait()
    again(a_in, hm, xm, HA, to_xp)
    again(b_in, hp, xp, HB, to_xm)
    s1.mid()
    z0cd.wait()
    again(ab3, hm, x, HB, to_xm)
    again(ab3, hp, x, HA, to_xp)
    again(a_in, hm, x, HB, to_xp)
    again(b_in, hp, x, HA, to_xm)
    c_og3.wait()
    s3.all()
    s0.end()
    s3.mid()

    def act_y(i):
        d = depths[i]
        own = ACT.at[d, ol, y, k] if i == 0 else ACT.at[d, :, y, k]
        y_pm[i].send(own, own, to_yp)
        y_pm[i].send(own, own, to_ym)

    y_f = [Group(ACT.at[d, :, 0, k]) for d in depths]
    c_act = [Group(ACT.at[d, :, pl.ds(0, 3), k]) for d in depths]

    def act_in(i):
        d = depths[i]
        y_pm[i].wait()
        y_f[i].send(ACT.at[d, 0, ym, k], ACT.at[d, 0, ym, k], to_yp)
        y_f[i].send(ACT.at[d, 1, yp, k], ACT.at[d, 1, yp, k], to_ym)
        for v in (ym, yp):
            c_act[i].send(ACT.at[d, :, v, k], ACT.at[d, :, v, k], to_core)

    def act_all(i):
        d = depths[i]
        y_f[i].wait()
        c_act[i].send(ACT.at[d, :, y2, k], ACT.at[d, :, y2, k], to_core)

    for d in d_act:
        d.wait()
    l_act.wait()
    act_y(0)
    act_y(1)
    act_y(2)
    c_own = send(ACT.at[:, :, y, k], ACT.at[:, :, y, k], to_core)
    ab3.wait()
    again(b_in, hp, xm, HA, to_xp)
    again(a_in, hm, xp, HB, to_xm)
    s0.out()
    s1.end()
    e13, e_in = Group(two_halves), Group(OG.at[h, pl.ds(0, 2)])
    z2ab.wait()
    again(e13, h2, x, HA, to_xp)
    again(e13, h2, x, HB, to_xm)
    again(e_in, h2, x, HA, to_xm)
    again(e_in, h2, x, HB, to_xp)
    act_in(0)
    s3.end()
    act_in(1)
    act_y(3)
    s1.out()
    act_in(2)
    e13.wait()
    again(e_in, h2, xm, HA, to_xp)
    again(e_in, h2, xp, HB, to_xm)
    act_all(0)
    c_own.wait()
    c_act[0].wait()
    wg(h, True)
    act_all(1)
    act_in(3)
    s3.out()
    a_in.wait()
    c_act[1].wait()
    wg(hm, False)
    act_all(2)
    b_in.wait()
    c_act[2].wait()
    act_all(3)
    wg(hp, False)
    e_in.wait()
    c_act[3].wait()
    wg(h2, False)
    for d in started:
        d.wait_send()


def body(activations, out_grad, weight):
    hbm = pl.BlockSpec(memory_space=pltpu.HBM)
    vmem = pl.BlockSpec(memory_space=pltpu.VMEM)
    input_grad, weight_grad = pl.pallas_call(
        kernel,
        out_shape=(pltpu.VMEM((192, 512), BF16), pltpu.VMEM((768, 1152), F32)),
        in_specs=[hbm] * 3,
        out_specs=(vmem, vmem),
        scratch_shapes=[
            pltpu.VMEM((2, 4, 192, 2304), BF16),
            pltpu.VMEM((4, 4, 128, 1152), BF16),
            pltpu.VMEM((4, 128, 1152), BF16),
            pltpu.VMEM((4, 2, 4, 2, 32, 768), BF16),
            pltpu.VMEM((4, 2, 4, 192, 128), F32),
            pltpu.VMEM((4, 2, 2, 96, 128), F32),
            pltpu.VMEM((4, 2, 2, 192, 128), F32),
            pltpu.VMEM((4, 192, 128), F32),
            pltpu.VMEM((4, 192, 128), F32),
            pltpu.VMEM((4, 192, 128), F32),
            pltpu.SemaphoreType.DMA((SEMS,)),
            pltpu.SemaphoreType.DMA((SEMS,)),
            pltpu.SemaphoreType.DMA((4,)),
        ],
        compiler_params=pltpu.CompilerParams(
            collective_id=0, has_side_effects=True, vmem_limit_bytes=48 * 1024 * 1024
        ),
        cost_estimate=pl.CostEstimate(flops=7_300_000_000, bytes_accessed=20_000_000, transcendentals=0),
    )(*[pltpu.with_memory_space_constraint(v, pltpu.HBM) for v in (activations, out_grad, weight.reshape(2, 4, 2, 192, 1152))])
    return input_grad.T, weight_grad.reshape(1, 1, 768, 1152)


def solution(mesh):
    return jax.shard_map(
        body,
        mesh=mesh,
        in_specs=(P(("depth", "col"), "row"), P(("depth", "row"), "col"), P("row", "col")),
        out_specs=(P("depth", ("row", "col")), P("row", "depth", None, "col")),
        check_vma=False,
    )
```
